256 devices in a mesh: expert: 128 (over y, x, z), shard: 2 (over core).
Axes of the slice: x: 4, y: 4, z: 8, core: 2. Of those that a mesh axis runs over, the one named last changes fastest.
Arguments:
- tokens: bfloat16 [32768, 2048], P(('expert', 'shard')), may hold values from -6 to 6
- router: bfloat16 [2048, 64], replicated, may hold values from -0.125 to 0.125
- w_gate: bfloat16 [128, 2048, 704], P('expert', None, 'shard'), may hold values from -0.125 to 0.125
- w_up: bfloat16 [128, 2048, 704], P('expert', None, 'shard'), may hold values from -0.125 to 0.125
- w_down: bfloat16 [128, 704, 2048], P('expert', 'shard'), may hold values from -0.15625 to 0.15625
- picks: int32 [256, 64, 8], P(('expert', 'shard')), may hold values from 0 to 127, as said below
- counts: int32 [256, 64], P(('expert', 'shard')), may hold values from 0 to 8, as said below
Outputs:
- mixed: bfloat16 [32768, 2048], P(('expert', 'shard'))
The draws below stay inside these ranges and needn't reach their ends.
Inputs may be any that keep to these rules, and one draw needn't show every extreme that they name: `picks`: within one source device and one expert the 8 entries are different tokens. `counts`: loads differ from expert to expert; in every draw some expert takes 8 tokens from every source device.
All inputs are finite; a program needn't handle non-finite values.
Results may differ from the reference program's by a relative error of at most 0.0057.
Values may be sent and summed in bfloat16 or wider, within the bound.
No kernel may reach another device: no remote copies, remote signals or barrier semaphores. Data moves between devices by JAX's collectives and lax.ppermute only.
A program may use at most 128 MiB of HBM per device.

```python
import jax
import jax.numpy as jnp
from jax import lax

D = 2048
FF = 1408
EXPERTS = 64
TOK_DEV = 128
SLOT = 8
SOURCES = 256
TOKENS = 32768


def draw_picks(key, part):
    scores = jax.random.randint(key, (SOURCES, EXPERTS, TOK_DEV), 0, 1 << 18) * TOK_DEV
    scores = scores + jnp.arange(TOK_DEV, dtype=jnp.int32)
    order = jnp.argsort(scores, axis=-1, stable=True)
    return order[:, :, :SLOT].astype(jnp.int32)


def draw_counts(key, part):
    key_floor, key_count, key_hot = jax.random.split(jax.random.fold_in(key, 7), 3)
    floors = jax.random.randint(key_floor, (EXPERTS,), 0, SLOT)
    drawn = jax.random.randint(key_count, (SOURCES, EXPERTS), floors[None, :], SLOT + 1)
    hottest = jax.random.randint(key_hot, (), 0, EXPERTS)
    column = jnp.arange(EXPERTS, dtype=jnp.int32)[None, :]
    return jnp.where(column == hottest, SLOT, drawn).astype(jnp.int32)


def block_levels(own_key, shape, shards, least, high):
    level = 1.0
    for axis_at, shards_of in shards:
        steps = jax.random.uniform(jax.random.fold_in(jax.random.fold_in(own_key, 6), axis_at), (shards_of,), jnp.float32, least / len(shards), high / len(shards))
        level = level * jnp.repeat(jnp.exp(steps), shape[axis_at] // shards_of).reshape((-1,) + (1,) * (len(shape) - 1 - axis_at))
    return level


def scatter_about(stream_key, dims, width, reach, cuts=(), kind=jnp.bfloat16):
    values = jax.random.normal(stream_key, dims, jnp.float32) * width
    if len(cuts) > 0:
        values = block_levels(stream_key, dims, cuts, -0.22, 0.18) * values
    return jnp.clip(values, min=-reach, max=reach).astype(kind)


def setup_inputs(seed: int = 0) -> dict:
    keys = jax.random.split(jax.random.key(seed), 8)
    return {
        "tokens": scatter_about(keys[0], (TOKENS, D), 1.0, 6.0, ((0, 256),)),
        "router": scatter_about(keys[1], (D, EXPERTS), D ** -0.5, 0.125),
        "w_gate": scatter_about(keys[2], (2 * EXPERTS, D, FF // 2), D ** -0.5, 0.125, ((0, 128), (2, 2))),
        "w_up": scatter_about(keys[3], (2 * EXPERTS, D, FF // 2), D ** -0.5, 0.125, ((0, 128), (2, 2))),
        "w_down": scatter_about(keys[4], (2 * EXPERTS, FF // 2, D), FF ** -0.5, 0.15625, ((0, 128), (1, 2))),
        "picks": draw_picks(jax.random.fold_in(keys[7], 71), 0),
        "counts": draw_counts(jax.random.fold_in(keys[7], 71), 0),
    }


def reference(tokens, router, w_gate, w_up, w_down, picks, counts):
    gate_values = jax.nn.sigmoid(jnp.dot(tokens, router, preferred_element_type=jnp.float32))
    offsets = (jnp.arange(SOURCES, dtype=jnp.int32) * TOK_DEV)[:, None]
    slot_index = jnp.arange(SLOT, dtype=jnp.int32)

    def expert_step(total, index):
        token_ids = (picks[:, index, :] + offsets).reshape(-1).astype(jnp.int32)
        gathered = tokens[token_ids]
        full_gate = jnp.concatenate([w_gate[2 * index], w_gate[2 * index + 1]], axis=1)
        full_up = jnp.concatenate([w_up[2 * index], w_up[2 * index + 1]], axis=1)
        full_down = jnp.concatenate([w_down[2 * index], w_down[2 * index + 1]], axis=0)
        gate_proj = jnp.dot(gathered, full_gate, preferred_element_type=jnp.float32)
        up_proj = jnp.dot(gathered, full_up, preferred_element_type=jnp.float32)
        hidden = (jax.nn.silu(gate_proj) * up_proj).astype(jnp.bfloat16)
        expert_out = jnp.dot(hidden, full_down, preferred_element_type=jnp.float32).astype(jnp.bfloat16)
        alive = (slot_index[None, :] < counts[:, index][:, None]).reshape(-1)
        weight = jnp.where(alive, gate_values[token_ids, index], jnp.zeros((), gate_values.dtype))
        total = total.at[token_ids].add(weight[:, None] * expert_out.astype(jnp.float32))
        return total, None

    start_total = jnp.zeros((TOKENS, D), jnp.float32)
    total, unused = lax.scan(expert_step, start_total, jnp.arange(EXPERTS, dtype=jnp.int32))
    return total.astype(jnp.bfloat16)
```

```python
import jax
import jax.numpy as jnp
from jax import lax
from jax.experimental import pallas as pl
from jax.experimental.pallas import tpu as pltpu
from jax.sharding import Mesh, PartitionSpec as P

YS, XS, ZS, CS = 4, 4, 8, 2
PLANE = YS * XS
NOTE = 8
NEAR = (0, -1, 1)
FAR = (-2, 2, -3, 3, 4)
ORDER = NEAR + FAR


def shift(block, axis, count, by):
    return lax.ppermute(block, axis, [(i, (i + by) % count) for i in range(count)])


def along_z(block, by):
    return shift(block, "z", ZS, by)


def ring_reduce(part):
    far = ZS // 2
    lines = []
    for half in (0, 1):
        for way in (1, -1):
            last = far if (half == 0) == (way == 1) else far - 1
            lines.append([half, way, last, None])
    for distance in range(far, 0, -1):
        for line in lines:
            half, way, last, moving = line
            if distance > last:
                continue
            mine = part(far if distance == far else way * distance, half)
            if moving is not None:
                mine = mine + moving.astype(jnp.float32)
            line[3] = along_z(mine.astype(jnp.bfloat16), way)
    halves = []
    for half in (0, 1):
        total = part(0, half)
        for line in lines:
            if line[0] == half:
                total = total + line[3].astype(jnp.float32)
        halves.append(total.astype(jnp.bfloat16))
    return jnp.concatenate(halves, axis=0)


def plane_exchange(rows):
    return lax.all_to_all(rows, ("y", "x"), split_axis=0, concat_axis=0, tiled=True)


TRANSPOSED = (((1,), (1,)), ((), ()))


def expert_kernel(column_ref, rows_ref, gate_ref, up_ref, down_ref, out_ref):
    rows = rows_ref[...]
    gate_proj = lax.dot_general(rows, gate_ref[...], TRANSPOSED, preferred_element_type=jnp.float32)
    up_proj = lax.dot_general(rows, up_ref[...], TRANSPOSED, preferred_element_type=jnp.float32)
    lane = lax.broadcasted_iota(jnp.int32, gate_proj.shape, 1)
    logit = jnp.sum(jnp.where(lane == column_ref[0], gate_proj, 0.0), axis=1, keepdims=True)
    weight = 1.0 / (1.0 + jnp.exp(-logit))
    hidden = (gate_proj / (1.0 + jnp.exp(-gate_proj)) * up_proj).astype(jnp.bfloat16)
    out = jnp.dot(hidden, down_ref[...], preferred_element_type=jnp.float32)
    out_ref[...] = (out * weight).astype(out_ref.dtype)


def expert_rows(column, rows, weights, block):
    count, width = rows.shape
    return pl.pallas_call(
        expert_kernel,
        grid=(count // block,),
        in_specs=[
            pl.BlockSpec(memory_space=pltpu.SMEM),
            pl.BlockSpec((block, width), lambda i: (i, 0)),
        ]
        + [pl.BlockSpec(memory_space=pltpu.VMEM)] * len(weights),
        out_specs=pl.BlockSpec((block, width), lambda i: (i, 0)),
        out_shape=jax.ShapeDtypeStruct((count, width), jnp.bfloat16),
        compiler_params=pltpu.CompilerParams(vmem_limit_bytes=28 * 1024 * 1024),
    )(column, rows, *weights)


def shards(tokens, router, w_gate, w_up, w_down, picks, counts):
    tok_count, width = tokens.shape
    half = tok_count // 2
    slots = picks.shape[2]
    zi = lax.axis_index("z")
    pair = zi // 2
    column = (lax.axis_index("y") * XS + lax.axis_index("x")) * (ZS // 2) + pair

    slot_of = lax.broadcasted_iota(jnp.int32, picks.shape[1:], 1)
    code = picks[0] + jnp.where(slot_of < counts[0][:, None], 0, tok_count)
    table = code.reshape(PLANE, ZS // 2, slots).transpose(1, 0, 2).reshape(ZS // 2, PLANE * slots)
    own_codes = lax.dynamic_index_in_dim(table, pair, axis=0, keepdims=False)
    note = jnp.pad(table.astype(jnp.bfloat16), ((0, NOTE - ZS // 2), (0, width - PLANE * slots)))

    first = jnp.concatenate([tokens[:half], note], axis=0)
    lines = {(0, 1): {0: first}, (0, -1): {0: first}, (1, 1): {0: tokens[half:]}, (1, -1): {0: tokens[half:]}}

    def advance(step):
        for (h, way), line in lines.items():
            if step < ZS // 2 or (h == 0) == (way == 1):
                line[step] = along_z(line[step - 1], way)

    def block_of(offset):
        if offset == 0:
            return tokens
        way = 1 if offset < 0 or offset == ZS // 2 else -1
        other = -1 if offset == ZS // 2 else way
        return jnp.concatenate([lines[0, way][abs(offset)][:half], lines[1, other][abs(offset)]], axis=0)

    known = {0: own_codes}

    def codes_of(offset):
        if offset not in known:
            way = 1 if offset < 0 or offset == ZS // 2 else -1
            found = lax.dynamic_slice(lines[0, way][abs(offset)], (half + pair, 0), (1, PLANE * slots))
            known[offset] = found[0].astype(jnp.int32)
        return known[offset]

    def both_cores(own, last):
        return jnp.concatenate([own, shift(own, "c", CS, 1), last], axis=0)

    below = router.T
    weights = (
        both_cores(w_gate[0].T, below),
        both_cores(w_up[0].T, jnp.zeros_like(below)),
        both_cores(w_down[0], jnp.zeros_like(below)),
    )

    token_id = lax.broadcasted_iota(jnp.int32, (1, tok_count), 1)

    def choose(offset):
        index = codes_of(offset) & (tok_count - 1)
        one_hot = (index[:, None] == token_id).astype(jnp.bfloat16)
        rows = jnp.dot(one_hot, block_of(offset), preferred_element_type=jnp.float32)
        return rows.astype(jnp.bfloat16).reshape(PLANE, slots, width)

    def pick_rows(group):
        return jnp.concatenate([choose(o) for o in group], axis=1)

    which = (column + weights[0].shape[0] - below.shape[0]).reshape(1)

    def feed_forward(rows, block):
        return expert_rows(which, rows.reshape(-1, width), weights, block).reshape(rows.shape)

    advance(1)
    advance(2)
    near_rows = plane_exchange(pick_rows(NEAR))
    advance(3)
    advance(4)
    near_rows, far_rows = lax.optimization_barrier((near_rows, pick_rows(FAR)))
    far_rows = plane_exchange(far_rows)
    near_out = feed_forward(near_rows, PLANE * slots * len(NEAR))
    near_out, far_rows = lax.optimization_barrier((near_out, far_rows))
    far_back = plane_exchange(feed_forward(far_rows, PLANE * slots * len(FAR) // 2))
    near_out, far_back = lax.optimization_barrier((near_out, far_back))
    near_back = plane_exchange(near_out)

    kept = lax.optimization_barrier({o: codes_of(o) for o in ORDER})

    def near_sums():
        code = jnp.stack([kept[o].reshape(PLANE, slots) for o in NEAR], axis=1).reshape(1, -1)
        row_of = lax.broadcasted_iota(jnp.int32, (1, code.shape[1]), 1) // slots % len(NEAR)
        place = jnp.where(code < tok_count, code + row_of * tok_count, -1)
        mine = place == lax.broadcasted_iota(jnp.int32, (len(NEAR) * tok_count, 1), 0)
        return jnp.dot(mine.astype(jnp.bfloat16), near_back.reshape(-1, width), preferred_element_type=jnp.float32)

    near_total = near_sums()

    def part(offset, h):
        if offset in NEAR:
            start = NEAR.index(offset) * tok_count + h * half
            return near_total[start : start + half]
        at = FAR.index(offset)
        rows = far_back[:, at * slots : (at + 1) * slots].reshape(PLANE * slots, width)
        mine = kept[offset][None, :] == lax.broadcasted_iota(jnp.int32, (half, 1), 0) + h * half
        return jnp.dot(mine.astype(jnp.bfloat16), rows, preferred_element_type=jnp.float32)

    return ring_reduce(part)


def solution(mesh):
    fine = Mesh(mesh.devices.reshape(YS, XS, ZS, CS), ("y", "x", "z", "c"))
    along = ("y", "x", "z")
    placed = (
        P((*along, "c"), None),
        P(),
        P(along, None, "c"),
        P(along, None, "c"),
        P(along, "c", None),
        P((*along, "c"), None, None),
        P((*along, "c"), None),
    )
    return jax.shard_map(
        shards, mesh=fine, in_specs=placed, out_specs=P((*along, "c"), None), check_vma=False
    )
```

```python
import jax
import jax.numpy as jnp
from jax import lax
from jax.experimental import pallas as pl
from jax.experimental.pallas import tpu as pltpu
from jax.sharding import Mesh, PartitionSpec as P

YS, XS, ZS, CS = 4, 4, 8, 2
PLANE = YS * XS
NOTE = 8
NEAR = (0, -1, 1)
FAR = (-2, 2, -3, 3, 4)
ORDER = NEAR + FAR


def shift(block, axis, count, by):
    return lax.ppermute(block, axis, [(i, (i + by) % count) for i in range(count)])


def along_z(block, by):
    return shift(block, "z", ZS, by)


def ring_reduce(part):
    far = ZS // 2
    lines = []
    for half in (0, 1):
        for way in (1, -1):
            last = far if (half == 0) == (way == 1) else far - 1
            lines.append([half, way, last, None])
    for distance in range(far, 0, -1):
        for line in lines:
            half, way, last, moving = line
            if distance > last:
                continue
            mine = part(far if distance == far else way * distance, half)
            if moving is not None:
                mine = mine + moving.astype(jnp.float32)
            line[3] = along_z(mine.astype(jnp.bfloat16), way)
    halves = []
    for half in (0, 1):
        total = part(0, half)
        for line in lines:
            if line[0] == half:
                total = total + line[3].astype(jnp.float32)
        halves.append(total.astype(jnp.bfloat16))
    return jnp.concatenate(halves, axis=0)


def plane_exchange(rows):
    return lax.all_to_all(rows, ("y", "x"), split_axis=0, concat_axis=0, tiled=True)


TRANSPOSED = (((1,), (1,)), ((), ()))


def expert_kernel(column_ref, rows_ref, gate_ref, up_ref, down_ref, out_ref):
    rows = rows_ref[...]
    gate_proj = lax.dot_general(rows, gate_ref[...], TRANSPOSED, preferred_element_type=jnp.float32)
    up_proj = lax.dot_general(rows, up_ref[...], TRANSPOSED, preferred_element_type=jnp.float32)
    lane = lax.broadcasted_iota(jnp.int32, gate_proj.shape, 1)
    logit = jnp.sum(jnp.where(lane == column_ref[0], gate_proj, 0.0), axis=1, keepdims=True)
    weight = 1.0 / (1.0 + jnp.exp(-logit))
    hidden = (gate_proj / (1.0 + jnp.exp(-gate_proj)) * up_proj).astype(jnp.bfloat16)
    out = jnp.dot(hidden, down_ref[...], preferred_element_type=jnp.float32)
    out_ref[...] = (out * weight).astype(out_ref.dtype)


def expert_rows(column, rows, weights, block):
    count, width = rows.shape
    return pl.pallas_call(
        expert_kernel,
        grid=(count // block,),
        in_specs=[
            pl.BlockSpec(memory_space=pltpu.SMEM),
            pl.BlockSpec((block, width), lambda i: (i, 0)),
        ]
        + [pl.BlockSpec(memory_space=pltpu.VMEM)] * len(weights),
        out_specs=pl.BlockSpec((block, width), lambda i: (i, 0)),
        out_shape=jax.ShapeDtypeStruct((count, width), jnp.bfloat16),
        compiler_params=pltpu.CompilerParams(vmem_limit_bytes=28 * 1024 * 1024),
    )(column, rows, *weights)


def shards(tokens, router, w_gate, w_up, w_down, picks, counts):
    tok_count, width = tokens.shape
    half = tok_count // 2
    slots = picks.shape[2]
    zi = lax.axis_index("z")
    pair = zi // 2
    column = (lax.axis_index("y") * XS + lax.axis_index("x")) * (ZS // 2) + pair

    slot_of = lax.broadcasted_iota(jnp.int32, picks.shape[1:], 1)
    code = picks[0] + jnp.where(slot_of < counts[0][:, None], 0, tok_count)
    table = code.reshape(PLANE, ZS // 2, slots).transpose(1, 0, 2).reshape(ZS // 2, PLANE * slots)
    own_codes = lax.dynamic_index_in_dim(table, pair, axis=0, keepdims=False)
    note = jnp.pad(table.astype(jnp.bfloat16), ((0, NOTE - ZS // 2), (0, width - PLANE * slots)))

    first = jnp.concatenate([tokens[:half], note], axis=0)
    lines = {(0, 1): {0: first}, (0, -1): {0: first}, (1, 1): {0: tokens[half:]}, (1, -1): {0: tokens[half:]}}

    def advance(step):
        for (h, way), line in lines.items():
            if step < ZS // 2 or (h == 0) == (way == 1):
                line[step] = along_z(line[step - 1], way)

    def block_of(offset):
        if offset == 0:
            return tokens
        way = 1 if offset < 0 or offset == ZS // 2 else -1
        other = -1 if offset == ZS // 2 else way
        return jnp.concatenate([lines[0, way][abs(offset)][:half], lines[1, other][abs(offset)]], axis=0)

    known = {0: own_codes}

    def codes_of(offset):
        if offset not in known:
            way = 1 if offset < 0 or offset == ZS // 2 else -1
            found = lax.dynamic_slice(lines[0, way][abs(offset)], (half + pair, 0), (1, PLANE * slots))
            known[offset] = found[0].astype(jnp.int32)
        return known[offset]

    def both_cores(own, last):
        return jnp.concatenate([own, shift(own, "c", CS, 1), last], axis=0)

    below = router.T
    weights = (
        both_cores(w_gate[0].T, below),
        both_cores(w_up[0].T, jnp.zeros_like(below)),
        both_cores(w_down[0], jnp.zeros_like(below)),
    )

    token_id = lax.broadcasted_iota(jnp.int32, (1, tok_count), 1)

    def choose(offset):
        index = codes_of(offset) & (tok_count - 1)
        one_hot = (index[:, None] == token_id).astype(jnp.bfloat16)
        rows = jnp.dot(one_hot, block_of(offset), preferred_element_type=jnp.float32)
        return rows.astype(jnp.bfloat16).reshape(PLANE, slots, width)

    def pick_rows(group):
        return jnp.concatenate([choose(o) for o in group], axis=1)

    which = (column + weights[0].shape[0] - below.shape[0]).reshape(1)

    def feed_forward(rows, block):
        return expert_rows(which, rows.reshape(-1, width), weights, block).reshape(rows.shape)

    advance(1)
    advance(2)
    near_rows = plane_exchange(pick_rows(NEAR))
    advance(3)
    advance(4)
    near_rows, far_rows = lax.optimization_barrier((near_rows, pick_rows(FAR)))
    far_rows = plane_exchange(far_rows)
    near_out = feed_forward(near_rows, PLANE * slots * len(NEAR))
    near_out, far_rows = lax.optimization_barrier((near_out, far_rows))
    far_back = plane_exchange(feed_forward(far_rows, PLANE * slots * len(FAR) // 2))
    near_out, far_back = lax.optimization_barrier((near_out, far_back))
    near_back = plane_exchange(near_out)

    kept = lax.optimization_barrier({o: codes_of(o) for o in ORDER})

    def combine(group, rows):
        code = jnp.stack([kept[o].reshape(PLANE, slots) for o in group], axis=1).reshape(1, -1)
        row_of = lax.broadcasted_iota(jnp.int32, (1, code.shape[1]), 1) // slots % len(group)
        place = jnp.where(code < tok_count, code + row_of * tok_count, -1)
        mine = place == lax.broadcasted_iota(jnp.int32, (len(group) * tok_count, 1), 0)
        return jnp.dot(mine.astype(jnp.bfloat16), rows.reshape(-1, width), preferred_element_type=jnp.float32)

    sums = {FAR: combine(FAR, far_back), NEAR: combine(NEAR, near_back)}

    def part(offset, h):
        group = FAR if offset in FAR else NEAR
        start = group.index(offset) * tok_count + h * half
        return sums[group][start : start + half]

    return ring_reduce(part)


def solution(mesh):
    fine = Mesh(mesh.devices.reshape(YS, XS, ZS, CS), ("y", "x", "z", "c"))
    along = ("y", "x", "z")
    placed = (
        P((*along, "c"), None),
        P(),
        P(along, None, "c"),
        P(along, None, "c"),
        P(along, "c", None),
        P((*along, "c"), None, None),
        P((*along, "c"), None),
    )
    return jax.shard_map(
        shards, mesh=fine, in_specs=placed, out_specs=P((*along, "c"), None), check_vma=False
    )
```

```python
import jax
import jax.numpy as jnp
from jax import lax
from jax.experimental import pallas as pl
from jax.experimental.pallas import tpu as pltpu
from jax.sharding import Mesh, PartitionSpec as P

YS, XS, ZS, CS = 4, 4, 8, 2
PLANE = YS * XS
NOTE = 8
NEAR = (0, -1, 1)
FAR = (-2, 2, -3, 3, 4)
ORDER = NEAR + FAR
MEET = 2


def shift(block, axis, count, by):
    return lax.ppermute(block, axis, [(i, (i + by) % count) for i in range(count)])


def along_z(block, by):
    return shift(block, "z", ZS, by)


def ring_reduce(part, meet):
    far = ZS // 2
    lines = []
    for half in (0, 1):
        for way in (1, -1):
            last = far if (half == 0) == (way == 1) else far - 1
            lines.append([half, way, last, None])
    for distance in range(far, 0, -1):
        if distance == MEET:
            for line, moving in zip(lines, meet([line[3] for line in lines])):
                line[3] = moving
        for line in lines:
            half, way, last, moving = line
            if distance > last:
                continue
            mine = part(far if distance == far else way * distance, half)
            if moving is not None:
                mine = mine + moving.astype(jnp.float32)
            line[3] = along_z(mine.astype(jnp.bfloat16), way)
    halves = []
    for half in (0, 1):
        total = part(0, half)
        for line in lines:
            if line[0] == half:
                total = total + line[3].astype(jnp.float32)
        halves.append(total.astype(jnp.bfloat16))
    return jnp.concatenate(halves, axis=0)


def plane_exchange(rows):
    return lax.all_to_all(rows, ("y", "x"), split_axis=0, concat_axis=0, tiled=True)


TRANSPOSED = (((1,), (1,)), ((), ()))


def expert_kernel(column_ref, rows_ref, gate_ref, up_ref, down_ref, out_ref):
    rows = rows_ref[...]
    gate_proj = lax.dot_general(rows, gate_ref[...], TRANSPOSED, preferred_element_type=jnp.float32)
    up_proj = lax.dot_general(rows, up_ref[...], TRANSPOSED, preferred_element_type=jnp.float32)
    lane = lax.broadcasted_iota(jnp.int32, gate_proj.shape, 1)
    logit = jnp.sum(jnp.where(lane == column_ref[0], gate_proj, 0.0), axis=1, keepdims=True)
    weight = 1.0 / (1.0 + jnp.exp(-logit))
    hidden = (gate_proj / (1.0 + jnp.exp(-gate_proj)) * up_proj).astype(jnp.bfloat16)
    out = jnp.dot(hidden, down_ref[...], preferred_element_type=jnp.float32)
    out_ref[...] = (out * weight).astype(out_ref.dtype)


def expert_rows(column, rows, weights, block):
    count, width = rows.shape
    return pl.pallas_call(
        expert_kernel,
        grid=(count // block,),
        in_specs=[
            pl.BlockSpec(memory_space=pltpu.SMEM),
            pl.BlockSpec((block, width), lambda i: (i, 0)),
        ]
        + [pl.BlockSpec(memory_space=pltpu.VMEM)] * len(weights),
        out_specs=pl.BlockSpec((block, width), lambda i: (i, 0)),
        out_shape=jax.ShapeDtypeStruct((count, width), jnp.bfloat16),
        compiler_params=pltpu.CompilerParams(vmem_limit_bytes=28 * 1024 * 1024),
    )(column, rows, *weights)


def shards(tokens, router, w_gate, w_up, w_down, picks, counts):
    tok_count, width = tokens.shape
    half = tok_count // 2
    slots = picks.shape[2]
    zi = lax.axis_index("z")
    pair = zi // 2
    column = (lax.axis_index("y") * XS + lax.axis_index("x")) * (ZS // 2) + pair

    slot_of = lax.broadcasted_iota(jnp.int32, picks.shape[1:], 1)
    code = picks[0] + jnp.where(slot_of < counts[0][:, None], 0, tok_count)
    table = code.reshape(PLANE, ZS // 2, slots).transpose(1, 0, 2).reshape(ZS // 2, PLANE * slots)
    own_codes = lax.dynamic_index_in_dim(table, pair, axis=0, keepdims=False)
    note = jnp.pad(table.astype(jnp.bfloat16), ((0, NOTE - ZS // 2), (0, width - PLANE * slots)))

    first = jnp.concatenate([tokens[:half], note], axis=0)
    lines = {(0, 1): {0: first}, (0, -1): {0: first}, (1, 1): {0: tokens[half:]}, (1, -1): {0: tokens[half:]}}

    def advance(step):
        for (h, way), line in lines.items():
            if step < ZS // 2 or (h == 0) == (way == 1):
                line[step] = along_z(line[step - 1], way)

    def block_of(offset):
        if offset == 0:
            return tokens
        way = 1 if offset < 0 or offset == ZS // 2 else -1
        other = -1 if offset == ZS // 2 else way
        return jnp.concatenate([lines[0, way][abs(offset)][:half], lines[1, other][abs(offset)]], axis=0)

    known = {0: own_codes}

    def codes_of(offset):
        if offset not in known:
            way = 1 if offset < 0 or offset == ZS // 2 else -1
            found = lax.dynamic_slice(lines[0, way][abs(offset)], (half + pair, 0), (1, PLANE * slots))
            known[offset] = found[0].astype(jnp.int32)
        return known[offset]

    def both_cores(own, last):
        return jnp.concatenate([own, shift(own, "c", CS, 1), last], axis=0)

    below = router.T
    weights = (
        both_cores(w_gate[0].T, below),
        both_cores(w_up[0].T, jnp.zeros_like(below)),
        both_cores(w_down[0], jnp.zeros_like(below)),
    )

    token_id = lax.broadcasted_iota(jnp.int32, (1, tok_count), 1)

    def choose(offset):
        index = codes_of(offset) & (tok_count - 1)
        one_hot = (index[:, None] == token_id).astype(jnp.bfloat16)
        rows = jnp.dot(one_hot, block_of(offset), preferred_element_type=jnp.float32)
        return rows.astype(jnp.bfloat16).reshape(PLANE, slots, width)

    def pick_rows(group):
        return jnp.concatenate([choose(o) for o in group], axis=1)

    which = (column + weights[0].shape[0] - below.shape[0]).reshape(1)

    def feed_forward(rows, block):
        return expert_rows(which, rows.reshape(-1, width), weights, block).reshape(rows.shape)

    advance(1)
    advance(2)
    near_rows = plane_exchange(pick_rows(NEAR))
    advance(3)
    advance(4)
    near_rows, far_rows = lax.optimization_barrier((near_rows, pick_rows(FAR)))
    far_rows = plane_exchange(far_rows)
    near_out = feed_forward(near_rows, PLANE * slots * len(NEAR))
    near_out, far_rows = lax.optimization_barrier((near_out, far_rows))
    far_back = plane_exchange(feed_forward(far_rows, PLANE * slots * len(FAR) // 2))
    near_out, far_back = lax.optimization_barrier((near_out, far_back))
    near_back = plane_exchange(near_out)

    kept = lax.optimization_barrier({o: codes_of(o) for o in ORDER})

    def combine(group, rows):
        code = jnp.stack([kept[o].reshape(PLANE, slots) for o in group], axis=1).reshape(1, -1)
        row_of = lax.broadcasted_iota(jnp.int32, (1, code.shape[1]), 1) // slots % len(group)
        place = jnp.where(code < tok_count, code + row_of * tok_count, -1)
        mine = place == lax.broadcasted_iota(jnp.int32, (len(group) * tok_count, 1), 0)
        return jnp.dot(mine.astype(jnp.bfloat16), rows.reshape(-1, width), preferred_element_type=jnp.float32)

    sums = {FAR: combine(FAR, far_back)}

    def meet(moving):
        moving, arrived = lax.optimization_barrier((moving, near_back))
        sums[NEAR] = combine(NEAR, arrived)
        return moving

    def part(offset, h):
        group = FAR if offset in FAR else NEAR
        start = group.index(offset) * tok_count + h * half
        return sums[group][start : start + half]

    return ring_reduce(part, meet)


def solution(mesh):
    fine = Mesh(mesh.devices.reshape(YS, XS, ZS, CS), ("y", "x", "z", "c"))
    along = ("y", "x", "z")
    placed = (
        P((*along, "c"), None),
        P(),
        P(along, None, "c"),
        P(along, None, "c"),
        P(along, "c", None),
        P((*along, "c"), None, None),
        P((*along, "c"), None),
    )
    return jax.shard_map(
        shards, mesh=fine, in_specs=placed, out_specs=P((*along, "c"), None), check_vma=False
    )
```
